32 devices in a mesh: seq: 8 (over z, x), head: 4 (over y, core).
Axes of the slice: x: 2, y: 2, z: 4, core: 2. Of those that a mesh axis runs over, the one named last changes fastest.
Arguments:
- query: bfloat16 [4, 4096, 128], P('head', 'seq'), may hold values from -8 to 8
- key: bfloat16 [4, 4096, 128], P('head', 'seq'), may hold values from -8 to 8
- value: bfloat16 [4, 4096, 128], P('head', 'seq'), may hold values from -16 to 16
- lin_query: bfloat16 [4, 4096, 128], P('head', 'seq'), may hold values from -52 to 52
- lin_key: bfloat16 [4, 4096, 128], P('head', 'seq'), may hold values from -5 to 5
- gain: float32 [4, 128], P('head'), may hold values from 0.25 to 1.75
- cotangent: bfloat16 [4, 4096, 128], P('head', 'seq'), may hold values from -16 to 16
- key_block: int32 [32, 20], replicated, may hold values from -1 to 31, as said below
Outputs:
- mixed: bfloat16 [4, 4096, 128], P('head', 'seq')
- grad_query: bfloat16 [4, 4096, 128], P('head', 'seq')
- grad_key: bfloat16 [4, 4096, 128], P('head', 'seq')
- grad_value: bfloat16 [4, 4096, 128], P('head', 'seq')
- grad_lin_query: bfloat16 [4, 4096, 128], P('head', 'seq')
- grad_lin_key: bfloat16 [4, 4096, 128], P('head', 'seq')
- grad_gain: float32 [4, 128], P('head')
The draws below stay inside these ranges and needn't reach their ends.
Inputs may be any that keep to these rules, and one draw needn't show every extreme that they name: `key_block`: row b lists the key blocks that query block b reads: slot 0 is b, slot 1 is b - 1 (-1 when b is 0); each later slot names a block that lies on an earlier index of seq than b and before b - 1, or is -1, and all -1 slots follow the named ones. A row names no block twice. Over all rows' slots from 2 on, at most one block of the blocks on one index of seq is named.
All inputs are finite; a program needn't handle non-finite values.
Results may differ from the reference program's by a relative error of at most 0.039.
Values may be sent and summed in bfloat16 or wider, within the bound.
A program may use at most 64 MiB of HBM per device.

```python
import math
import jax
import jax.numpy as jnp
from jax import lax

HEAD_DIM = 128
TOK_DEV = 512
BLK = 128
SEL = 20
HEADS = 4
TOKENS = 4096
NBLK = 32


def score_pair(key):
    base = jax.random.fold_in(key, 11)
    key_q, key_k = jax.random.split(base, 2)
    shape = (HEADS, TOKENS, HEAD_DIM)
    queries = jnp.clip(jax.random.normal(key_q, shape, jnp.float32), -6.0, 6.0)
    keys = jnp.clip(jax.random.normal(key_k, shape, jnp.float32), -6.0, 6.0)
    return (queries, keys)


def draw_query(key, part):
    return score_pair(key)[0].astype(jnp.bfloat16)


def draw_key(key, part):
    return score_pair(key)[1].astype(jnp.bfloat16)


def draw_value(key, part):
    key_v, key_c = jax.random.split(jax.random.fold_in(key, 23))
    shape = (HEADS, TOKENS, HEAD_DIM)
    column = jnp.exp(jax.random.uniform(key_c, (HEADS, 1, HEAD_DIM), jnp.float32, 0.0, math.log(10.0))) / 3.0
    basic = jnp.clip(jax.random.normal(key_v, shape, jnp.float32), -4.0, 4.0)
    return jnp.clip(basic * column, -16.0, 16.0).astype(jnp.bfloat16)


def draw_lin_query(key, part):
    key_v, key_r = jax.random.split(jax.random.fold_in(key, 31))
    shape = (HEADS, TOKENS, HEAD_DIM)
    row = jnp.exp(jax.random.uniform(key_r, (HEADS, TOKENS, 1), jnp.float32, 0.0, math.log(10.0))) / 3.0
    factor = 1.0 + 2.0 * jnp.arange(HEADS).astype(jnp.float32) / max(HEADS - 1, 1)
    basic = jnp.clip(jax.random.normal(key_v, shape, jnp.float32), -4.0, 4.0)
    return jnp.clip(basic * row * factor[:, None, None], -52.0, 52.0).astype(jnp.bfloat16)


def draw_cotangent(key, part):
    key_v = jax.random.fold_in(key, 41)
    shape = (HEADS, TOKENS, HEAD_DIM)
    ramp = 1.0 + 2.0 * jnp.arange(TOKENS).astype(jnp.float32) / TOKENS
    basic = jnp.clip(jax.random.normal(key_v, shape, jnp.float32), -4.0, 4.0)
    return jnp.clip(basic * ramp[None, :, None], -16.0, 16.0).astype(jnp.bfloat16)


def draw_key_block(key, part):
    per_dev = TOK_DEV // BLK
    owners = NBLK // per_dev
    key_c, key_s = jax.random.split(jax.random.fold_in(key, 5))
    chosen = jax.random.randint(key_c, (owners,), 0, per_dev) + jnp.arange(owners) * per_dev
    rows = jnp.arange(NBLK)
    owner = rows // per_dev
    places = jnp.arange(owners)
    valid = (places[None, :] < owner[:, None]) & (chosen[None, :] < rows[:, None] - 1)
    score = jax.random.randint(key_s, (NBLK, owners), 0, 1 << 20) * owners + places[None, :]
    score = jnp.where(valid, score, -1 - places[None, :])
    picks = min(SEL - 2, owners)
    top_score, top_place = lax.top_k(score, picks)
    far = jnp.where(top_score >= 0, chosen[top_place], -1)
    if SEL - 2 > picks:
        far = jnp.concatenate([far, jnp.full((NBLK, SEL - 2 - picks), -1, far.dtype)], axis=1)
    local = jnp.stack([rows, rows - 1], axis=1)
    return jnp.concatenate([local, far], axis=1).astype(jnp.int32)


def shard_levels(rng, extent, pieces, smallest, top_value):
    factor_of, own = 1.0, jax.random.fold_in(rng, 6)
    for dim, shards_of in pieces:
        heights = jnp.exp(jax.random.uniform(jax.random.fold_in(own, dim), (shards_of,), jnp.float32, smallest / len(pieces), top_value / len(pieces)))
        factor_of = factor_of * jnp.repeat(heights, extent[dim] // shards_of).reshape([-1 if axis == dim else 1 for axis in range(len(extent))])
    return factor_of


def gaussian(own_key, dims, deviation, reach, shards=(), kind=jnp.bfloat16):
    array = jax.random.normal(own_key, dims, jnp.float32) * deviation
    if len(shards) > 0:
        array = shard_levels(own_key, dims, shards, -0.22, 0.18) * array
    return jnp.clip(array, min=-reach, max=reach).astype(kind)


def setup_inputs(seed: int = 0) -> dict:
    key_list = jax.random.split(jax.random.key(seed), 9)
    return {
        "query": draw_query(jax.random.fold_in(key_list[8], 71), 0),
        "key": draw_key(jax.random.fold_in(key_list[8], 71), 0),
        "value": draw_value(jax.random.fold_in(key_list[8], 71), 0),
        "lin_query": draw_lin_query(jax.random.fold_in(key_list[8], 71), 0),
        "lin_key": gaussian(key_list[4], (HEADS, TOKENS, HEAD_DIM), 1.0, 5.0, ((0, 4), (1, 8))),
        "gain": jnp.clip(1.0 + 0.15 * jax.random.normal(key_list[5], (HEADS, HEAD_DIM), jnp.float32), 0.25, 1.75),
        "cotangent": draw_cotangent(jax.random.fold_in(key_list[8], 71), 0),
        "key_block": draw_key_block(jax.random.fold_in(key_list[8], 71), 0),
    }


masked_value = -1e+30
eps_norm = 1e-05

def allowed_rows(names):
    live = names >= 0
    causal = jnp.arange(BLK)[:, None] >= jnp.arange(BLK)[None, :]
    first = jnp.arange(SEL) == 0
    return live[None, :, None] & (jnp.logical_not(first)[None, :, None] | causal[:, None, :])

def reference(query, key, value, lin_query, lin_key, gain, cotangent, key_block):
    f32 = jnp.float32
    bf16 = jnp.bfloat16
    hi = lax.Precision.HIGHEST
    heads = query.shape[0]
    scale = HEAD_DIM ** (-0.5)
    features = heads * HEAD_DIM

    def blocks(x):
        return x.reshape(heads, NBLK, BLK, HEAD_DIM).transpose(1, 0, 2, 3)

    def unblocks(x):
        return x.transpose(1, 0, 2, 3).reshape(heads, TOKENS, HEAD_DIM)
    query_b = blocks(query)
    key_b = blocks(key)
    value_b = blocks(value)
    order = jnp.arange(NBLK, dtype=jnp.int32)

    def scores_of(b):
        names = key_block[b]
        index = jnp.maximum(names, 0).astype(jnp.int32)
        rows_q = query_b[b].astype(f32)
        keys_g = key_b[index].astype(f32)
        values_g = value_b[index].astype(f32)
        scores = jnp.einsum('hqd,jhkd->hqjk', rows_q, keys_g, precision=hi) * scale
        scores = jnp.where(allowed_rows(names)[None], scores, masked_value)
        return (index, rows_q, keys_g, values_g, scores)

    def attend(b):
        index, rows_q, keys_g, values_g, scores = scores_of(b)
        row_max = lax.optimization_barrier(jnp.max(scores, axis=(2, 3), keepdims=True))
        weights = jnp.exp(scores - row_max)
        total = lax.optimization_barrier(jnp.sum(weights, axis=(2, 3), keepdims=True))
        weights_b = lax.optimization_barrier(weights.astype(bf16)).astype(f32)
        summed = jnp.einsum('hqjk,jhkd->hqd', weights_b, values_g, precision=hi)
        attended = (summed / total[..., 0]).astype(bf16)
        log_total = (row_max + jnp.log(total))[..., 0, 0]
        return (attended, log_total)
    attended, log_total = lax.map(attend, order)
    att_f = attended.astype(f32)
    lq_all = blocks(lin_query).astype(f32)
    lk_all = blocks(lin_key).astype(f32)
    lower = (jnp.arange(BLK)[:, None] >= jnp.arange(BLK)[None, :]).astype(f32)
    zero_state = jnp.zeros((heads, HEAD_DIM, HEAD_DIM), f32)

    def run(state, piece):
        lq, lk, vo = piece
        mixing = jnp.einsum('hqi,hki->hqk', lq, lk, precision=hi) * lower
        out = jnp.einsum('hqk,hkd->hqd', mixing, vo, precision=hi) + jnp.einsum('hqi,hij->hqj', lq, state, precision=hi)
        return (state + jnp.einsum('hki,hkj->hij', lk, vo, precision=hi), (out, state))
    final_state, (linear, prior) = lax.scan(run, zero_state, (lq_all, lk_all, att_f))
    squares = lax.optimization_barrier(jnp.sum(linear * linear, axis=(1, 3)))
    inv_rms = lax.rsqrt(squares / features + eps_norm)
    normed = linear * inv_rms[:, None, :, None]
    mixed = (att_f + gain[None, :, None, :] * normed).astype(bf16)
    grad_out = blocks(cotangent).astype(f32)
    grad_gain = lax.optimization_barrier(jnp.sum(grad_out * normed, axis=(0, 2)))
    scaled = grad_out * gain[None, :, None, :]
    inner = lax.optimization_barrier(jnp.sum(scaled * normed, axis=(1, 3)))
    grad_linear = inv_rms[:, None, :, None] * (scaled - normed * (inner / features)[:, None, :, None])

    def back(after, piece):
        lq, lk, vo, glin, before = piece
        mixing = jnp.einsum('hqi,hki->hqk', lq, lk, precision=hi) * lower
        pairs = jnp.einsum('hqd,hkd->hqk', glin, vo, precision=hi) * lower
        g_lq = jnp.einsum('hqk,hki->hqi', pairs, lk, precision=hi) + jnp.einsum('hqj,hij->hqi', glin, before, precision=hi)
        g_lk = jnp.einsum('hqk,hqi->hki', pairs, lq, precision=hi) + jnp.einsum('hkj,hij->hki', vo, after, precision=hi)
        g_att = jnp.einsum('hqk,hqd->hkd', mixing, glin, precision=hi) + jnp.einsum('hki,hij->hkj', lk, after, precision=hi)
        return (after + jnp.einsum('hti,htj->hij', lq, glin, precision=hi), (g_lq, g_lk, g_att))
    first_state, (g_lq, g_lk, g_att) = lax.scan(back, zero_state, (lq_all, lk_all, att_f, grad_linear, prior), reverse=True)
    grad_att = (grad_out + g_att).astype(bf16)
    grad_att_f = grad_att.astype(f32)
    delta = lax.optimization_barrier(jnp.sum(grad_att_f * att_f, axis=3))

    def grads(carry, b):
        acc_key, acc_value = carry
        index, rows_q, keys_g, values_g, scores = scores_of(b)
        probs = jnp.exp(scores - log_total[b][..., None, None])
        probs_b = lax.optimization_barrier(probs.astype(bf16)).astype(f32)
        go = grad_att_f[b]
        grad_probs = jnp.einsum('hqd,jhkd->hqjk', go, values_g, precision=hi)
        grad_scores = probs * (grad_probs - delta[b][..., None, None])
        grad_scores = lax.optimization_barrier(grad_scores.astype(bf16)).astype(f32)
        gq = (jnp.einsum('hqjk,jhkd->hqd', grad_scores, keys_g, precision=hi) * scale).astype(bf16)
        gk = jnp.einsum('hqjk,hqd->jhkd', grad_scores, rows_q, precision=hi) * scale
        gv = jnp.einsum('hqjk,hqd->jhkd', probs_b, go, precision=hi)
        return ((acc_key.at[index].add(gk), acc_value.at[index].add(gv)), gq)
    zero_grads = jnp.zeros((NBLK, heads, BLK, HEAD_DIM), f32)
    (acc_key, acc_value), grad_q = lax.scan(grads, (zero_grads, zero_grads), order)
    return (unblocks(mixed), unblocks(grad_q), unblocks(acc_key.astype(bf16)), unblocks(acc_value.astype(bf16)), unblocks(g_lq.astype(bf16)), unblocks(g_lk.astype(bf16)), grad_gain)
```

```python
import functools

import jax
import jax.numpy as jnp
from jax import lax
from jax.experimental import pallas as pl
from jax.experimental.pallas import tpu as pltpu
from jax.sharding import PartitionSpec as P

BLK = 128
masked_value = -1e30
eps_norm = 1e-05
f32 = jnp.float32
bf16 = jnp.bfloat16
MESH = pl.DeviceIdType.MESH


def parts(x):
    if x.dtype == bf16:
        return (x,)
    high = x.astype(bf16)
    return (high, (x - high.astype(f32)).astype(bf16))


def dot(a, b, ca, cb):
    return lax.dot_general(a, b, (((ca,), (cb,)), ((), ())), preferred_element_type=f32)


def mm(a, b, ca, cb):
    pa, pb = parts(a), parts(b)
    out = None
    for i, x in enumerate(pa):
        for j, y in enumerate(pb):
            if i + j < 2:
                term = dot(x, y, ca, cb)
                out = term if out is None else out + term
    return out


def loop(low, high, body):
    def step(i, carry):
        body(i)
        return carry

    lax.fori_loop(low, high, step, jnp.int32(0))


def kernel(
    n, nh, scale,
    q, k, v, lq, lk, gain, cot, kbs, kbv,
    mixed, gq, gk, gv, glq, glk, gg,
    kvsend, kvbuf, kvext, stsend, stbuf, grsend, grbuf, hsend, hbuf, ggsend, ggbuf,
    gfsend, gfbuf, gbsend, gbbuf, att, wn, wf, dsf, pbf, mix,
    kv_s, kv_r, pv_s, pv_r, st_s, st_r, gr_s, gr_r, h_s, h_r, gg_s, gg_r, gf_s, gf_r, gb_s, gb_r,
):
    rows, width = q.shape
    blk = BLK
    per_dev = rows // blk
    me = lax.axis_index("seq")
    hd = lax.axis_index("head")
    features = nh * width

    barrier = pltpu.get_barrier_semaphore()

    def greet(d):
        pl.semaphore_signal(barrier, inc=1, device_id={"seq": d}, device_id_type=MESH)

    def greet_head(d):
        pl.semaphore_signal(barrier, inc=1, device_id={"head": d}, device_id_type=MESH)

    loop(0, me, greet)
    loop(me + 1, n, greet)
    loop(0, hd, greet_head)
    loop(hd + 1, nh, greet_head)

    def link(src, dst, ssem, rsem, axis, d):
        return pltpu.make_async_remote_copy(
            src_ref=src, dst_ref=dst, send_sem=ssem, recv_sem=rsem,
            device_id={axis: d}, device_id_type=MESH,
        )

    base = me * per_dev
    names = kbv[...]
    slot = lax.broadcasted_iota(jnp.int32, names.shape, 1)
    ours = (slot >= 2) & (names >= base) & (names < base + per_dev)
    local = jnp.where(ours, names - base, 0).astype(f32)
    mine = jnp.max(jnp.max(local, axis=1, keepdims=True), axis=0, keepdims=True)
    for side, ref in ((0, k), (1, v)):
        chosen = ref[0:blk, :].astype(f32)
        for g in range(1, per_dev):
            chosen = jnp.where(mine == g, ref[g * blk : (g + 1) * blk, :].astype(f32), chosen)
        kvsend[side] = chosen.astype(bf16)
        kvext[side, blk : blk + rows, :] = ref[...]

    pl.semaphore_wait(barrier, n - 1 + nh - 1)

    def kv_copy(slot_at, peer):
        return link(kvsend, kvbuf.at[:, slot_at], kv_s.at[peer], kv_r.at[slot_at], "seq", peer)

    def prev_copy(peer):
        return link(
            kvext.at[:, rows : rows + blk], kvext.at[:, 0:blk], pv_s, pv_r, "seq", peer
        )

    @pl.when(me < n - 1)
    def _():
        prev_copy(me + 1).start()

    loop(me + 1, n, lambda d: kv_copy(me, d).start())

    @pl.when(me == 0)
    def _():
        kvext[:, 0:blk, :] = jnp.zeros((2, blk, width), bf16)

    def clear(d):
        kvbuf[:, pl.ds(d, 1)] = jnp.zeros((2, 1, blk, width), bf16)

    loop(me, n, clear)

    tri = lax.broadcasted_iota(jnp.int32, (rows, rows), 0) >= lax.broadcasted_iota(
        jnp.int32, (rows, rows), 1
    )
    mix[...] = jnp.where(tri, dot(lq[...], lk[...], 1, 1), 0.0)

    @pl.when(me > 0)
    def _():
        prev_copy(me - 1).wait_recv()

    loop(0, me, lambda s: kv_copy(s, s).wait_recv())

    kfar = kvbuf[0].reshape(n * blk, width)
    vfar = kvbuf[1].reshape(n * blk, width)

    row_i = lax.broadcasted_iota(jnp.int32, (blk, 2 * blk), 0)
    col_i = lax.broadcasted_iota(jnp.int32, (blk, 2 * blk), 1)
    causal = (col_i >= blk) & (col_i - blk <= row_i)
    first = lax.broadcasted_iota(jnp.int32, (1, n * blk), 1) // blk * per_dev
    inv_total = []
    for g in range(per_dev):
        at = slice(g * blk, (g + 1) * blk)
        near = slice(g * blk, (g + 2) * blk)
        qg = q[at, :]
        reach = blk if g else jnp.where(me > 0, blk, 0)
        sn = jnp.where(causal | (col_i < reach), dot(qg, kvext[0, near, :], 1, 1) * scale, masked_value)
        hit = jnp.zeros((1, n * blk), jnp.int32)
        for j in range(2, kbs.shape[1]):
            name = kbs[base + g, j]
            hit = jnp.maximum(
                hit, jnp.where((first <= name) & (name < first + per_dev), 1, 0)
            )
        sf = jnp.where(hit > 0, dot(qg, kfar, 1, 1) * scale, masked_value)
        top = jnp.maximum(
            jnp.max(sn, axis=1, keepdims=True), jnp.max(sf, axis=1, keepdims=True)
        )
        en = jnp.exp(sn - top)
        ef = jnp.exp(sf - top)
        total = jnp.sum(en, axis=1, keepdims=True) + jnp.sum(ef, axis=1, keepdims=True)
        summed = dot(en.astype(bf16), kvext[1, near, :], 1, 0) + dot(ef.astype(bf16), vfar, 1, 0)
        att[at, :] = (summed / total).astype(bf16)
        wn[at, :] = en
        wf[at, :] = ef
        inv_total.append(1.0 / total)

    stsend[...] = dot(lk[...], att[...], 0, 0)

    def st_copy(slot_at, peer):
        return link(stsend, stbuf.at[slot_at], st_s.at[peer], st_r.at[slot_at], "seq", peer)

    loop(me + 1, n, lambda d: st_copy(me, d).start())
    linear = mm(mix[...], att[...], 1, 0)

    def take_state(s, acc):
        st_copy(s, s).wait_recv()
        return acc + stbuf[s]

    prior = lax.fori_loop(0, me, take_state, jnp.zeros((width, width), f32))
    linear = linear + mm(lq[...], prior, 1, 0)
    co = cot[...].astype(f32)
    scaled = co * gain[...]
    ones = jnp.ones((8, width), bf16)
    hsend[0:8, :] = mm(ones, linear * linear, 1, 1)
    hsend[8:16, :] = mm(ones, scaled * linear, 1, 1)

    def h_copy(slot_at, peer):
        return link(hsend, hbuf.at[slot_at], h_s.at[peer], h_r.at[slot_at], "head", peer)

    loop(0, hd, lambda d: h_copy(hd, d).start())
    loop(hd + 1, nh, lambda d: h_copy(hd, d).start())

    def take_head(s, acc):
        h_copy(s, s).wait_recv()
        return acc + hbuf[s]

    heads = lax.fori_loop(0, hd, take_head, hsend[...])
    heads = lax.fori_loop(hd + 1, nh, take_head, heads)
    spread = jnp.full((8, width), 0.125, bf16)
    squares = mm(heads[0:8, :], spread, 0, 0)
    crossed = mm(heads[8:16, :], spread, 0, 0)
    inv_rms = lax.rsqrt(squares / features + eps_norm)
    normed = linear * inv_rms
    a32 = att[...].astype(f32)
    grad_linear = inv_rms * (scaled - normed * (crossed * inv_rms / features))

    grsend[...] = mm(lq[...], grad_linear, 0, 0)

    def gr_copy(slot_at, peer):
        return link(grsend, grbuf.at[slot_at], gr_s.at[peer], gr_r.at[slot_at], "seq", peer)

    loop(0, me, lambda d: gr_copy(me, d).start())
    ggsend[...] = jnp.broadcast_to(jnp.sum(co * normed, axis=0, keepdims=True), (8, width))

    def gg_copy(slot_at, peer):
        return link(ggsend, ggbuf.at[slot_at], gg_s.at[peer], gg_r.at[slot_at], "seq", peer)

    loop(0, me, lambda d: gg_copy(me, d).start())
    loop(me + 1, n, lambda d: gg_copy(me, d).start())

    mixed[...] = (a32 + gain[...] * normed).astype(bf16)
    pairs = jnp.where(tri, mm(grad_linear, att[...], 1, 1), 0.0)
    glq[...] = (mm(pairs, lk[...], 1, 0) + mm(grad_linear, prior, 1, 1)).astype(bf16)
    grad_lk = mm(pairs, lq[...], 0, 0)
    grad_att = co + mm(mix[...], grad_linear, 0, 0)

    def take_grad(s, acc):
        gr_copy(s, s).wait_recv()
        return acc + grbuf[s]

    later = lax.fori_loop(me + 1, n, take_grad, jnp.zeros((width, width), f32))
    glk[...] = (grad_lk + mm(att[...], later, 1, 1)).astype(bf16)
    grad_att = (grad_att + mm(lk[...], later, 1, 0)).astype(bf16)
    delta = jnp.sum(grad_att.astype(f32) * a32, axis=1, keepdims=True)

    for g in range(per_dev):
        at = slice(g * blk, (g + 1) * blk)
        pf = wf[at, :] * inv_total[g]
        pbf[at, :] = pf.astype(bf16)
        dsf[at, :] = (pf * (dot(grad_att[at, :], vfar, 1, 1) - delta[at, :])).astype(bf16)
    gfsend[0] = (dot(dsf[...], q[...], 0, 0) * scale).astype(bf16).reshape(n, blk, width)
    gfsend[1] = dot(pbf[...], grad_att, 0, 0).astype(bf16).reshape(n, blk, width)

    def gf_copy(slot_at, peer):
        return link(
            gfsend.at[:, peer], gfbuf.at[:, slot_at], gf_s.at[peer], gf_r.at[slot_at], "seq", peer
        )

    loop(0, me, lambda d: gf_copy(me, d).start())

    key_terms = [None] * (per_dev + 1)
    value_terms = [None] * (per_dev + 1)

    def put(terms, i, x):
        terms[i] = x if terms[i] is None else terms[i] + x

    def gb_copy(peer):
        return link(gbsend, gbbuf, gb_s, gb_r, "seq", peer)

    for g in range(per_dev):
        at = slice(g * blk, (g + 1) * blk)
        near = slice(g * blk, (g + 2) * blk)
        pn = wn[at, :] * inv_total[g]
        ga = grad_att[at, :]
        ds = (pn * (dot(ga, kvext[1, near, :], 1, 1) - delta[at, :])).astype(bf16)
        nk = dot(ds, q[at, :], 0, 0) * scale
        nv = dot(pn.astype(bf16), ga, 0, 0)
        for i in range(2):
            half = slice(i * blk, (i + 1) * blk)
            put(key_terms, g + i, nk[half, :])
            put(value_terms, g + i, nv[half, :])
        if g == 0:
            gbsend[0] = key_terms[0].astype(bf16)
            gbsend[1] = value_terms[0].astype(bf16)

            @pl.when(me > 0)
            def _():
                gb_copy(me - 1).start()

        gq[at, :] = (
            (dot(ds, kvext[0, near, :], 1, 0) + dot(dsf[at, :], kfar, 1, 0)) * scale
        ).astype(bf16)

    def take_gain(s, acc):
        gg_copy(s, s).wait_recv()
        return acc + ggbuf[s]

    gains = lax.fori_loop(0, me, take_gain, ggsend[...])
    gains = lax.fori_loop(me + 1, n, take_gain, gains)
    gg[...] = gains[0:1, :]

    @pl.when(me == n - 1)
    def _():
        gbbuf[...] = jnp.zeros_like(gbbuf)

    @pl.when(me < n - 1)
    def _():
        gb_copy(me + 1).wait_recv()

    zero = jnp.zeros((blk, width), f32)

    def take_far(s, acc):
        gf_copy(s, s).wait_recv()
        return (acc[0] + gfbuf[0, s].astype(f32), acc[1] + gfbuf[1, s].astype(f32))

    far = lax.fori_loop(me + 1, n, take_far, (zero, zero))
    for side, (terms, out) in enumerate(((key_terms, gk), (value_terms, gv))):
        for g in range(per_dev):
            x = terms[g + 1] + jnp.where(mine == g, far[side], 0.0)
            if g == per_dev - 1:
                x = x + gbbuf[side].astype(f32)
            out[g * blk : (g + 1) * blk, :] = x.astype(bf16)

    @pl.when(me < n - 1)
    def _():
        prev_copy(me + 1).wait_send()

    @pl.when(me > 0)
    def _():
        gb_copy(me - 1).wait_send()

    def sent_up(d):
        kv_copy(me, d).wait_send()
        st_copy(me, d).wait_send()
        gg_copy(me, d).wait_send()

    def sent_down(d):
        gr_copy(me, d).wait_send()
        gf_copy(me, d).wait_send()
        gg_copy(me, d).wait_send()

    loop(me + 1, n, sent_up)
    loop(0, me, sent_down)
    loop(0, hd, lambda d: h_copy(hd, d).wait_send())
    loop(hd + 1, nh, lambda d: h_copy(hd, d).wait_send())


def per_device(query, key, value, lin_query, lin_key, gain, cotangent, key_block):
    heads, rows, width = query.shape
    n = lax.axis_size("seq")
    nh = lax.axis_size("head")
    blk = BLK
    flat = lambda x: x.reshape(heads * rows, width)
    vm = pl.BlockSpec(memory_space=pltpu.VMEM)
    big = jax.ShapeDtypeStruct((rows, width), bf16)
    dma = pltpu.SemaphoreType.DMA
    outs = pl.pallas_call(
        functools.partial(kernel, n, nh, width ** (-0.5)),
        out_shape=[big] * 6 + [jax.ShapeDtypeStruct((1, width), f32)],
        in_specs=[vm] * 7 + [pl.BlockSpec(memory_space=pltpu.SMEM), vm],
        out_specs=[vm] * 7,
        scratch_shapes=[
            pltpu.VMEM((2, blk, width), bf16),
            pltpu.VMEM((2, n, blk, width), bf16),
            pltpu.VMEM((2, rows + blk, width), bf16),
            pltpu.VMEM((width, width), f32),
            pltpu.VMEM((n, width, width), f32),
            pltpu.VMEM((width, width), f32),
            pltpu.VMEM((n, width, width), f32),
            pltpu.VMEM((16, rows), f32),
            pltpu.VMEM((nh, 16, rows), f32),
            pltpu.VMEM((8, width), f32),
            pltpu.VMEM((n, 8, width), f32),
            pltpu.VMEM((2, n, blk, width), bf16),
            pltpu.VMEM((2, n, blk, width), bf16),
            pltpu.VMEM((2, blk, width), bf16),
            pltpu.VMEM((2, blk, width), bf16),
            pltpu.VMEM((rows, width), bf16),
            pltpu.VMEM((rows, 2 * blk), f32),
            pltpu.VMEM((rows, n * blk), f32),
            pltpu.VMEM((rows, n * blk), bf16),
            pltpu.VMEM((rows, n * blk), bf16),
            pltpu.VMEM((rows, rows), f32),
            dma((n,)), dma((n,)), dma, dma,
            dma((n,)), dma((n,)), dma((n,)), dma((n,)),
            dma((nh,)), dma((nh,)), dma((n,)), dma((n,)),
            dma((n,)), dma((n,)), dma, dma,
        ],
        compiler_params=pltpu.CompilerParams(
            collective_id=0, has_side_effects=True, vmem_limit_bytes=56 * 2**20
        ),
    )(
        flat(query), flat(key), flat(value), flat(lin_query), flat(lin_key), gain,
        flat(cotangent), key_block, key_block,
    )
    return tuple(x.reshape(heads, rows, width) for x in outs[:6]) + (outs[6],)


def solution(mesh):
    split = P("head", "seq", None)
    return jax.shard_map(
        per_device,
        mesh=mesh,
        in_specs=(split,) * 5 + (P("head", None), split, P()),
        out_specs=(split,) * 6 + (P("head", None),),
        check_vma=False,
    )
```

```python
import functools

import jax
import jax.numpy as jnp
from jax import lax
from jax.experimental import pallas as pl
from jax.experimental.pallas import tpu as pltpu
from jax.sharding import PartitionSpec as P

BLK = 128
masked_value = -1e30
eps_norm = 1e-05
f32 = jnp.float32
bf16 = jnp.bfloat16
MESH = pl.DeviceIdType.MESH


def parts(x):
    if x.dtype == bf16:
        return (x,)
    high = x.astype(bf16)
    return (high, (x - high.astype(f32)).astype(bf16))


def dot(a, b, ca, cb):
    return lax.dot_general(a, b, (((ca,), (cb,)), ((), ())), preferred_element_type=f32)


def mm(a, b, ca, cb):
    pa, pb = parts(a), parts(b)
    out = None
    for i, x in enumerate(pa):
        for j, y in enumerate(pb):
            if i + j < 2:
                term = dot(x, y, ca, cb)
                out = term if out is None else out + term
    return out


def loop(low, high, body):
    def step(i, carry):
        body(i)
        return carry

    lax.fori_loop(low, high, step, jnp.int32(0))


def kernel(
    n, nh, scale,
    q, k, v, lq, lk, gain, cot, kbs, kbv,
    out, gg,
    kvsend, kvbuf, kvext, stsend, stbuf, grsend, grbuf, hsend, hbuf, ggsend, ggbuf,
    gfsend, gfbuf, gbsend, gbbuf, att, wn, wf, dsf, pbf, mix,
    kv_s, kv_r, pv_s, pv_r, st_s, st_r, gr_s, gr_r, h_s, h_r, gg_s, gg_r, gf_s, gf_r, gb_s, gb_r,
):
    rows, width = q.shape
    blk = BLK
    per_dev = rows // blk
    me = lax.axis_index("seq")
    hd = lax.axis_index("head")
    features = nh * width
    mixed, gq, gk, gv, glq, glk = (out.at[i] for i in range(6))

    barrier = pltpu.get_barrier_semaphore()

    def greet(d):
        pl.semaphore_signal(barrier, inc=1, device_id={"seq": d}, device_id_type=MESH)

    def greet_head(d):
        pl.semaphore_signal(barrier, inc=1, device_id={"head": d}, device_id_type=MESH)

    loop(0, me, greet)
    loop(me + 1, n, greet)
    loop(0, hd, greet_head)
    loop(hd + 1, nh, greet_head)

    def link(src, dst, ssem, rsem, axis, d):
        return pltpu.make_async_remote_copy(
            src_ref=src, dst_ref=dst, send_sem=ssem, recv_sem=rsem,
            device_id={axis: d}, device_id_type=MESH,
        )

    base = me * per_dev
    names = kbv[...]
    slot = lax.broadcasted_iota(jnp.int32, names.shape, 0)
    ours = (slot >= 2) & (names >= base) & (names < base + per_dev)
    local = jnp.where(ours, names - base, 0).astype(f32)
    mine = jnp.max(jnp.max(local, axis=1, keepdims=True), axis=0, keepdims=True)
    for side, ref in ((0, k), (1, v)):
        chosen = ref[0:blk, :].astype(f32)
        for g in range(1, per_dev):
            chosen = jnp.where(mine == g, ref[g * blk : (g + 1) * blk, :].astype(f32), chosen)
        kvsend[side] = chosen.astype(bf16)
        kvext[side, blk : blk + rows, :] = ref[...]

    pl.semaphore_wait(barrier, n - 1 + nh - 1)

    def kv_copy(side, slot_at, peer):
        return link(
            kvsend.at[side], kvbuf.at[side, slot_at], kv_s.at[side, peer], kv_r.at[side, slot_at],
            "seq", peer,
        )

    def prev_copy(peer):
        return link(
            kvext.at[:, rows : rows + blk], kvext.at[:, 0:blk], pv_s, pv_r, "seq", peer
        )

    @pl.when(me < n - 1)
    def _():
        prev_copy(me + 1).start()

    loop(0, n - 1 - me, lambda i: kv_copy(0, me, n - 1 - i).start())
    loop(0, n - 1 - me, lambda i: kv_copy(1, me, n - 1 - i).start())

    @pl.when(me == 0)
    def _():
        kvext[:, 0:blk, :] = jnp.zeros((2, blk, width), bf16)

    def clear(d):
        kvbuf[:, pl.ds(d, 1)] = jnp.zeros((2, 1, blk, width), bf16)

    loop(me, n, clear)

    tri = lax.broadcasted_iota(jnp.int32, (rows, rows), 0) >= lax.broadcasted_iota(
        jnp.int32, (rows, rows), 1
    )
    mix[...] = jnp.where(tri, dot(lq[...], lk[...], 1, 1), 0.0)

    row_i = lax.broadcasted_iota(jnp.int32, (blk, 2 * blk), 0)
    col_i = lax.broadcasted_iota(jnp.int32, (blk, 2 * blk), 1)
    causal = (col_i >= blk) & (col_i - blk <= row_i)

    def near_scores(g):
        at = slice(g * blk, (g + 1) * blk)
        near = slice(g * blk, (g + 2) * blk)
        reach = blk if g else jnp.where(me > 0, blk, 0)
        wn[at, :] = jnp.where(
            causal | (col_i < reach), dot(q[at, :], kvext[0, near, :], 1, 1) * scale, masked_value
        )

    for g in range(1, per_dev):
        near_scores(g)

    @pl.when(me > 0)
    def _():
        prev_copy(me - 1).wait_recv()

    near_scores(0)
    loop(0, me, lambda s: kv_copy(0, s, s).wait_recv())
    kfar = kvbuf[0].reshape(n * blk, width)
    first = lax.broadcasted_iota(jnp.int32, (1, n * blk), 1) // blk * per_dev
    inv_total = []
    near_sum = []
    for g in range(per_dev):
        at = slice(g * blk, (g + 1) * blk)
        near = slice(g * blk, (g + 2) * blk)
        hit = jnp.zeros((1, n * blk), jnp.int32)
        for j in range(2, kbs.shape[0]):
            name = kbs[j, base + g]
            hit = jnp.maximum(
                hit, jnp.where((first <= name) & (name < first + per_dev), 1, 0)
            )
        sn = wn[at, :]
        sf = jnp.where(hit > 0, dot(q[at, :], kfar, 1, 1) * scale, masked_value)
        top = jnp.maximum(
            jnp.max(sn, axis=1, keepdims=True), jnp.max(sf, axis=1, keepdims=True)
        )
        en = jnp.exp(sn - top)
        ef = jnp.exp(sf - top)
        total = jnp.sum(en, axis=1, keepdims=True) + jnp.sum(ef, axis=1, keepdims=True)
        inv_total.append(1.0 / total)
        near_sum.append(dot(en.astype(bf16), kvext[1, near, :], 1, 0))
        wn[at, :] = en
        wf[at, :] = ef
        pbf[at, :] = ef.astype(bf16)

    loop(0, me, lambda s: kv_copy(1, s, s).wait_recv())
    vfar = kvbuf[1].reshape(n * blk, width)
    far_sum = dot(pbf[...], vfar, 1, 0)
    for g in range(per_dev):
        at = slice(g * blk, (g + 1) * blk)
        att[at, :] = ((near_sum[g] + far_sum[at, :]) * inv_total[g]).astype(bf16)

    stsend[...] = dot(lk[...], att[...], 0, 0).astype(bf16)

    def st_copy(slot_at, peer):
        return link(stsend, stbuf.at[slot_at], st_s.at[peer], st_r.at[slot_at], "seq", peer)

    loop(0, n - 1 - me, lambda i: st_copy(me, n - 1 - i).start())
    linear = mm(mix[...], att[...], 1, 0)

    def take_state(s, acc):
        st_copy(s, s).wait_recv()
        return acc + stbuf[s].astype(f32)

    prior = lax.fori_loop(0, me, take_state, jnp.zeros((width, width), f32))
    linear = linear + mm(lq[...], prior, 1, 0)
    co = cot[...].astype(f32)
    scaled = co * gain[...]
    ones = jnp.ones((8, width), bf16)
    upper = lax.broadcasted_iota(jnp.int32, (8, 1), 0) < 4
    hsend[...] = jnp.where(
        upper, mm(ones, linear * linear, 1, 1), mm(ones, scaled * linear, 1, 1)
    )

    def h_copy(slot_at, peer):
        return link(hsend, hbuf.at[slot_at], h_s.at[peer], h_r.at[slot_at], "head", peer)

    loop(0, hd, lambda d: h_copy(hd, d).start())
    loop(hd + 1, nh, lambda d: h_copy(hd, d).start())

    def take_head(s, acc):
        h_copy(s, s).wait_recv()
        return acc + hbuf[s]

    heads = lax.fori_loop(0, hd, take_head, hsend[...])
    heads = lax.fori_loop(hd + 1, nh, take_head, heads)
    half = lax.broadcasted_iota(jnp.int32, (8, width), 0) < 4
    squares = mm(heads, jnp.where(half, 0.25, 0.0).astype(bf16), 0, 0)
    crossed = mm(heads, jnp.where(half, 0.0, 0.25).astype(bf16), 0, 0)
    inv_rms = lax.rsqrt(squares / features + eps_norm)
    normed = linear * inv_rms
    a32 = att[...].astype(f32)
    grad_linear = inv_rms * (scaled - normed * (crossed * inv_rms / features))

    grsend[...] = mm(lq[...], grad_linear, 0, 0).astype(bf16)

    def gr_copy(slot_at, peer):
        return link(grsend, grbuf.at[slot_at], gr_s.at[peer], gr_r.at[slot_at], "seq", peer)

    loop(0, me, lambda d: gr_copy(me, d).start())
    ggsend[...] = jnp.broadcast_to(jnp.sum(co * normed, axis=0, keepdims=True), (8, width))

    def gg_copy(slot_at, peer):
        return link(ggsend, ggbuf.at[slot_at], gg_s.at[peer], gg_r.at[slot_at], "seq", peer)

    loop(0, me, lambda d: gg_copy(me, d).start())
    loop(me + 1, n, lambda d: gg_copy(me, d).start())

    grad_att = co + mm(mix[...], grad_linear, 0, 0)
    pairs = jnp.where(tri, mm(grad_linear, att[...], 1, 1), 0.0)
    mix[...] = pairs
    glq[...] = (mm(pairs, lk[...], 1, 0) + mm(grad_linear, prior, 1, 1)).astype(bf16)
    for g in range(per_dev):
        at = slice(g * blk, (g + 1) * blk)
        pf = wf[at, :] * inv_total[g]
        wf[at, :] = pf
        pbf[at, :] = pf.astype(bf16)

    def take_grad(s, acc):
        gr_copy(s, s).wait_recv()
        return acc + grbuf[s].astype(f32)

    later = lax.fori_loop(me + 1, n, take_grad, jnp.zeros((width, width), f32))
    grad_att = (grad_att + mm(lk[...], later, 1, 0)).astype(bf16)
    delta = jnp.sum(grad_att.astype(f32) * a32, axis=1, keepdims=True)

    def gf_copy(side, slot_at, peer):
        return link(
            gfsend.at[side, peer], gfbuf.at[side, slot_at], gf_s.at[side, peer],
            gf_r.at[side, slot_at], "seq", peer,
        )

    gfsend[1] = dot(pbf[...], grad_att, 0, 0).astype(bf16).reshape(n, blk, width)
    loop(0, me, lambda d: gf_copy(1, me, d).start())
    for g in range(per_dev):
        at = slice(g * blk, (g + 1) * blk)
        dsf[at, :] = (wf[at, :] * (dot(grad_att[at, :], vfar, 1, 1) - delta[at, :])).astype(bf16)
    gfsend[0] = (dot(dsf[...], q[...], 0, 0) * scale).astype(bf16).reshape(n, blk, width)
    loop(0, me, lambda d: gf_copy(0, me, d).start())

    key_terms = [None] * (per_dev + 1)
    value_terms = [None] * (per_dev + 1)

    def put(terms, i, x):
        terms[i] = x if terms[i] is None else terms[i] + x

    def gb_copy(peer):
        return link(gbsend, gbbuf, gb_s, gb_r, "seq", peer)

    for g in range(per_dev):
        at = slice(g * blk, (g + 1) * blk)
        near = slice(g * blk, (g + 2) * blk)
        pn = wn[at, :] * inv_total[g]
        ga = grad_att[at, :]
        ds = (pn * (dot(ga, kvext[1, near, :], 1, 1) - delta[at, :])).astype(bf16)
        nk = dot(ds, q[at, :], 0, 0) * scale
        nv = dot(pn.astype(bf16), ga, 0, 0)
        for i in range(2):
            half = slice(i * blk, (i + 1) * blk)
            put(key_terms, g + i, nk[half, :])
            put(value_terms, g + i, nv[half, :])
        if g == 0:
            gbsend[0] = key_terms[0].astype(bf16)
            gbsend[1] = value_terms[0].astype(bf16)

            @pl.when(me > 0)
            def _():
                gb_copy(me - 1).start()

        gq[at, :] = (
            (dot(ds, kvext[0, near, :], 1, 0) + dot(dsf[at, :], kfar, 1, 0)) * scale
        ).astype(bf16)

    glk[...] = (mm(mix[...], lq[...], 0, 0) + mm(att[...], later, 1, 1)).astype(bf16)
    mixed[...] = (a32 + gain[...] * normed).astype(bf16)

    def take_gain(s, acc):
        gg_copy(s, s).wait_recv()
        return acc + ggbuf[s]

    gains = lax.fori_loop(0, me, take_gain, ggsend[...])
    gains = lax.fori_loop(me + 1, n, take_gain, gains)
    gg[...] = gains[0:1, :]

    @pl.when(me == n - 1)
    def _():
        gbbuf[...] = jnp.zeros_like(gbbuf)

    @pl.when(me < n - 1)
    def _():
        gb_copy(me + 1).wait_recv()

    zero = jnp.zeros((blk, width), f32)

    for side, terms, result in ((1, value_terms, gv), (0, key_terms, gk)):

        def take_far(s, acc):
            gf_copy(side, s, s).wait_recv()
            return acc + gfbuf[side, s].astype(f32)

        far = lax.fori_loop(me + 1, n, take_far, zero)
        for g in range(per_dev):
            x = terms[g + 1] + jnp.where(mine == g, far, 0.0)
            if g == per_dev - 1:
                x = x + gbbuf[side].astype(f32)
            result[g * blk : (g + 1) * blk, :] = x.astype(bf16)

    @pl.when(me < n - 1)
    def _():
        prev_copy(me + 1).wait_send()

    @pl.when(me > 0)
    def _():
        gb_copy(me - 1).wait_send()

    def sent_up(d):
        kv_copy(0, me, d).wait_send()
        kv_copy(1, me, d).wait_send()
        st_copy(me, d).wait_send()
        gg_copy(me, d).wait_send()

    def sent_down(d):
        gr_copy(me, d).wait_send()
        gf_copy(0, me, d).wait_send()
        gf_copy(1, me, d).wait_send()
        gg_copy(me, d).wait_send()

    loop(me + 1, n, sent_up)
    loop(0, me, sent_down)
    loop(0, hd, lambda d: h_copy(hd, d).wait_send())
    loop(hd + 1, nh, lambda d: h_copy(hd, d).wait_send())


def hand_out(stacked, gains, *refs):
    sems = refs[7]
    copies = [
        pltpu.make_async_copy(stacked.at[pl.ds(i, 1)], refs[i], sems.at[i]) for i in range(6)
    ]
    copies.append(pltpu.make_async_copy(gains, refs[6], sems.at[6]))
    for copy in copies:
        copy.start()
    for copy in copies:
        copy.wait()


def per_device(query, key, value, lin_query, lin_key, gain, cotangent, key_block):
    heads, rows, width = query.shape
    n = lax.axis_size("seq")
    nh = lax.axis_size("head")
    blk = BLK
    flat = lambda x: x.reshape(heads * rows, width)
    vm = pl.BlockSpec(memory_space=pltpu.VMEM)
    hbm = pl.BlockSpec(memory_space=pl.ANY)
    total = jax.ShapeDtypeStruct((1, width), f32)
    dma = pltpu.SemaphoreType.DMA
    stacked, gains = pl.pallas_call(
        functools.partial(kernel, n, nh, width ** (-0.5)),
        out_shape=[jax.ShapeDtypeStruct((6, rows, width), bf16), total],
        in_specs=[vm] * 7 + [pl.BlockSpec(memory_space=pltpu.SMEM), vm],
        out_specs=[vm] * 2,
        scratch_shapes=[
            pltpu.VMEM((2, blk, width), bf16),
            pltpu.VMEM((2, n, blk, width), bf16),
            pltpu.VMEM((2, rows + blk, width), bf16),
            pltpu.VMEM((width, width), bf16),
            pltpu.VMEM((n, width, width), bf16),
            pltpu.VMEM((width, width), bf16),
            pltpu.VMEM((n, width, width), bf16),
            pltpu.VMEM((8, rows), f32),
            pltpu.VMEM((nh, 8, rows), f32),
            pltpu.VMEM((8, width), f32),
            pltpu.VMEM((n, 8, width), f32),
            pltpu.VMEM((2, n, blk, width), bf16),
            pltpu.VMEM((2, n, blk, width), bf16),
            pltpu.VMEM((2, blk, width), bf16),
            pltpu.VMEM((2, blk, width), bf16),
            pltpu.VMEM((rows, width), bf16),
            pltpu.VMEM((rows, 2 * blk), f32),
            pltpu.VMEM((rows, n * blk), f32),
            pltpu.VMEM((rows, n * blk), bf16),
            pltpu.VMEM((rows, n * blk), bf16),
            pltpu.VMEM((rows, rows), f32),
            dma((2, n)), dma((2, n)), dma, dma,
            dma((n,)), dma((n,)), dma((n,)), dma((n,)),
            dma((nh,)), dma((nh,)), dma((n,)), dma((n,)),
            dma((2, n)), dma((2, n)), dma, dma,
        ],
        compiler_params=pltpu.CompilerParams(
            collective_id=0, has_side_effects=True, vmem_limit_bytes=56 * 2**20
        ),
    )(
        flat(query), flat(key), flat(value), flat(lin_query), flat(lin_key), gain,
        flat(cotangent), key_block.T, key_block.T,
    )
    return tuple(
        pl.pallas_call(
            hand_out,
            out_shape=[jax.ShapeDtypeStruct((heads, rows, width), bf16)] * 6 + [total],
            in_specs=[hbm] * 2,
            out_specs=[hbm] * 7,
            scratch_shapes=[dma((7,))],
        )(stacked, gains)
    )


def solution(mesh):
    split = P("head", "seq", None)
    return jax.shard_map(
        per_device,
        mesh=mesh,
        in_specs=(split,) * 5 + (P("head", None), split, P()),
        out_specs=(split,) * 6 + (P("head", None),),
        check_vma=False,
    )
```

```python
import functools

import jax
import jax.numpy as jnp
from jax import lax
from jax.experimental import pallas as pl
from jax.experimental.pallas import tpu as pltpu
from jax.sharding import PartitionSpec as P

BLK = 128
masked_value = -1e30
eps_norm = 1e-05
f32 = jnp.float32
bf16 = jnp.bfloat16
MESH = pl.DeviceIdType.MESH


def parts(x):
    if x.dtype == bf16:
        return (x,)
    high = x.astype(bf16)
    return (high, (x - high.astype(f32)).astype(bf16))


def dot(a, b, ca, cb):
    return lax.dot_general(a, b, (((ca,), (cb,)), ((), ())), preferred_element_type=f32)


def mm(a, b, ca, cb):
    pa, pb = parts(a), parts(b)
    out = None
    for i, x in enumerate(pa):
        for j, y in enumerate(pb):
            if i + j < 2:
                term = dot(x, y, ca, cb)
                out = term if out is None else out + term
    return out


def loop(low, high, body):
    def step(i, carry):
        body(i)
        return carry

    lax.fori_loop(low, high, step, jnp.int32(0))


def kernel(
    n, nh, scale,
    q, k, v, lq, lk, gain, cot, kbs, kbv,
    out, gg,
    kvsend, kvbuf, kvext, stsend, stbuf, grsend, grbuf, hsend, hbuf, ggsend, ggbuf,
    gfsend, gfbuf, gbsend, gbbuf, att, wn, wf, dsf, pbf, mix,
    kv_s, kv_r, pv_s, pv_r, st_s, st_r, gr_s, gr_r, h_s, h_r, gg_s, gg_r, gf_s, gf_r, gb_s, gb_r, fw_s,
):
    rows, width = q.shape
    blk = BLK
    per_dev = rows // blk
    me = lax.axis_index("seq")
    hd = lax.axis_index("head")
    features = nh * width
    mixed, gq, gk, gv, glq, glk = (out.at[i] for i in range(6))

    barrier = pltpu.get_barrier_semaphore()

    def greet(d):
        pl.semaphore_signal(barrier, inc=1, device_id={"seq": d}, device_id_type=MESH)

    def greet_head(d):
        pl.semaphore_signal(barrier, inc=1, device_id={"head": d}, device_id_type=MESH)

    loop(0, me, greet)
    loop(me + 1, n, greet)
    loop(0, hd, greet_head)
    loop(hd + 1, nh, greet_head)

    def link(src, dst, ssem, rsem, axis, d):
        return pltpu.make_async_remote_copy(
            src_ref=src, dst_ref=dst, send_sem=ssem, recv_sem=rsem,
            device_id={axis: d}, device_id_type=MESH,
        )

    base = me * per_dev
    names = kbv[...]
    slot = lax.broadcasted_iota(jnp.int32, names.shape, 0)
    ours = (slot >= 2) & (names >= base) & (names < base + per_dev)
    local = jnp.where(ours, names - base, 0).astype(f32)
    mine = jnp.max(jnp.max(local, axis=1, keepdims=True), axis=0, keepdims=True)
    for side, ref in ((0, k), (1, v)):
        chosen = ref[0:blk, :].astype(f32)
        for g in range(1, per_dev):
            chosen = jnp.where(mine == g, ref[g * blk : (g + 1) * blk, :].astype(f32), chosen)
        kvsend[side] = chosen.astype(bf16)
        kvext[side, blk : blk + rows, :] = ref[...]

    pl.semaphore_wait(barrier, n - 1 + nh - 1)

    def kv_copy(side, slot_at, peer):
        return link(
            kvsend.at[side], kvbuf.at[side, slot_at], kv_s.at[side, peer], kv_r.at[side, slot_at],
            "seq", peer,
        )

    def prev_copy(peer):
        return link(
            kvext.at[:, rows : rows + blk], kvext.at[:, 0:blk], pv_s, pv_r, "seq", peer
        )

    @pl.when(me < n - 1)
    def _():
        prev_copy(me + 1).start()

    odd = me % 2
    pair = me // 2
    ahead = n // 2 - 1 - pair
    partner = me + 1 - 2 * odd

    def kv_pass(side, s):
        return link(
            kvbuf.at[side, s], kvbuf.at[side, s], fw_s.at[side, s], kv_r.at[side, s],
            "seq", partner,
        )

    def kv_take(side):
        def take_and_pass(i):
            s = me - 2 - 2 * i
            kv_copy(side, s, s).wait_recv()
            kv_pass(side, s).start()

        loop(0, pair, take_and_pass)

    def kv_rest(side):
        def take(i):
            s = 1 - odd + 2 * i
            kv_copy(side, s, s).wait_recv()

        loop(0, pair + odd, take)

    for side in range(2):
        loop(0, ahead, lambda i: kv_copy(side, me, me + 2 * (ahead - i)).start())

        @pl.when(odd == 0)
        def _():
            kv_copy(side, me, me + 1).start()

    @pl.when(me == 0)
    def _():
        kvext[:, 0:blk, :] = jnp.zeros((2, blk, width), bf16)

    def clear(d):
        kvbuf[:, pl.ds(d, 1)] = jnp.zeros((2, 1, blk, width), bf16)

    loop(me, n, clear)

    tri = lax.broadcasted_iota(jnp.int32, (rows, rows), 0) >= lax.broadcasted_iota(
        jnp.int32, (rows, rows), 1
    )
    mix[...] = jnp.where(tri, dot(lq[...], lk[...], 1, 1), 0.0)

    row_i = lax.broadcasted_iota(jnp.int32, (blk, 2 * blk), 0)
    col_i = lax.broadcasted_iota(jnp.int32, (blk, 2 * blk), 1)
    causal = (col_i >= blk) & (col_i - blk <= row_i)

    def near_scores(g):
        at = slice(g * blk, (g + 1) * blk)
        near = slice(g * blk, (g + 2) * blk)
        reach = blk if g else jnp.where(me > 0, blk, 0)
        wn[at, :] = jnp.where(
            causal | (col_i < reach), dot(q[at, :], kvext[0, near, :], 1, 1) * scale, masked_value
        )

    for g in range(1, per_dev):
        near_scores(g)

    @pl.when(me > 0)
    def _():
        prev_copy(me - 1).wait_recv()

    near_scores(0)
    kv_take(0)
    kv_rest(0)
    kfar = kvbuf[0].reshape(n * blk, width)
    first = lax.broadcasted_iota(jnp.int32, (1, n * blk), 1) // blk * per_dev
    kv_take(1)
    inv_total = []
    near_sum = []
    for g in range(per_dev):
        at = slice(g * blk, (g + 1) * blk)
        near = slice(g * blk, (g + 2) * blk)
        hit = jnp.zeros((1, n * blk), jnp.int32)
        for j in range(2, kbs.shape[0]):
            name = kbs[j, base + g]
            hit = jnp.maximum(
                hit, jnp.where((first <= name) & (name < first + per_dev), 1, 0)
            )
        sn = wn[at, :]
        sf = jnp.where(hit > 0, dot(q[at, :], kfar, 1, 1) * scale, masked_value)
        top = jnp.maximum(
            jnp.max(sn, axis=1, keepdims=True), jnp.max(sf, axis=1, keepdims=True)
        )
        en = jnp.exp(sn - top)
        ef = jnp.exp(sf - top)
        total = jnp.sum(en, axis=1, keepdims=True) + jnp.sum(ef, axis=1, keepdims=True)
        inv_total.append(1.0 / total)
        near_sum.append(dot(en.astype(bf16), kvext[1, near, :], 1, 0))
        wn[at, :] = en
        wf[at, :] = ef
        pbf[at, :] = ef.astype(bf16)

    kv_rest(1)
    vfar = kvbuf[1].reshape(n * blk, width)
    far_sum = dot(pbf[...], vfar, 1, 0)
    for g in range(per_dev):
        at = slice(g * blk, (g + 1) * blk)
        att[at, :] = ((near_sum[g] + far_sum[at, :]) * inv_total[g]).astype(bf16)

    stsend[...] = dot(lk[...], att[...], 0, 0).astype(bf16)

    def st_copy(slot_at, peer):
        return link(stsend, stbuf.at[slot_at], st_s.at[peer], st_r.at[slot_at], "seq", peer)

    loop(0, n - 1 - me, lambda i: st_copy(me, n - 1 - i).start())
    linear = mm(mix[...], att[...], 1, 0)

    def take_state(s, acc):
        st_copy(s, s).wait_recv()
        return acc + stbuf[s].astype(f32)

    prior = lax.fori_loop(0, me, take_state, jnp.zeros((width, width), f32))
    linear = linear + mm(lq[...], prior, 1, 0)
    co = cot[...].astype(f32)
    scaled = co * gain[...]
    ones = jnp.ones((8, width), bf16)
    upper = lax.broadcasted_iota(jnp.int32, (8, 1), 0) < 4
    hsend[...] = jnp.where(
        upper, mm(ones, linear * linear, 1, 1), mm(ones, scaled * linear, 1, 1)
    )

    def h_copy(slot_at, peer):
        return link(hsend, hbuf.at[slot_at], h_s.at[peer], h_r.at[slot_at], "head", peer)

    loop(0, hd, lambda d: h_copy(hd, d).start())
    loop(hd + 1, nh, lambda d: h_copy(hd, d).start())

    def take_head(s, acc):
        h_copy(s, s).wait_recv()
        return acc + hbuf[s]

    heads = lax.fori_loop(0, hd, take_head, hsend[...])
    heads = lax.fori_loop(hd + 1, nh, take_head, heads)
    half = lax.broadcasted_iota(jnp.int32, (8, width), 0) < 4
    squares = mm(heads, jnp.where(half, 0.25, 0.0).astype(bf16), 0, 0)
    crossed = mm(heads, jnp.where(half, 0.0, 0.25).astype(bf16), 0, 0)
    inv_rms = lax.rsqrt(squares / features + eps_norm)
    normed = linear * inv_rms
    a32 = att[...].astype(f32)
    grad_linear = inv_rms * (scaled - normed * (crossed * inv_rms / features))

    grsend[...] = mm(lq[...], grad_linear, 0, 0).astype(bf16)

    def gr_copy(slot_at, peer):
        return link(grsend, grbuf.at[slot_at], gr_s.at[peer], gr_r.at[slot_at], "seq", peer)

    loop(0, me, lambda d: gr_copy(me, d).start())
    ggsend[...] = jnp.broadcast_to(jnp.sum(co * normed, axis=0, keepdims=True), (8, width))

    def gg_copy(slot_at, peer):
        return link(ggsend, ggbuf.at[slot_at], gg_s.at[peer], gg_r.at[slot_at], "seq", peer)

    loop(0, me, lambda d: gg_copy(me, d).start())
    loop(me + 1, n, lambda d: gg_copy(me, d).start())

    grad_att = co + mm(mix[...], grad_linear, 0, 0)
    pairs = jnp.where(tri, mm(grad_linear, att[...], 1, 1), 0.0)
    mix[...] = pairs
    glq[...] = (mm(pairs, lk[...], 1, 0) + mm(grad_linear, prior, 1, 1)).astype(bf16)
    for g in range(per_dev):
        at = slice(g * blk, (g + 1) * blk)
        pf = wf[at, :] * inv_total[g]
        wf[at, :] = pf
        pbf[at, :] = pf.astype(bf16)

    def take_grad(s, acc):
        gr_copy(s, s).wait_recv()
        return acc + grbuf[s].astype(f32)

    later = lax.fori_loop(me + 1, n, take_grad, jnp.zeros((width, width), f32))
    grad_att = (grad_att + mm(lk[...], later, 1, 0)).astype(bf16)
    delta = jnp.sum(grad_att.astype(f32) * a32, axis=1, keepdims=True)

    def gf_copy(side, slot_at, peer):
        return link(
            gfsend.at[side, peer], gfbuf.at[side, slot_at], gf_s.at[side, peer],
            gf_r.at[side, slot_at], "seq", peer,
        )

    gfsend[1] = dot(pbf[...], grad_att, 0, 0).astype(bf16).reshape(n, blk, width)
    loop(0, me, lambda d: gf_copy(1, me, d).start())
    for g in range(per_dev):
        at = slice(g * blk, (g + 1) * blk)
        dsf[at, :] = (wf[at, :] * (dot(grad_att[at, :], vfar, 1, 1) - delta[at, :])).astype(bf16)
    gfsend[0] = (dot(dsf[...], q[...], 0, 0) * scale).astype(bf16).reshape(n, blk, width)
    loop(0, me, lambda d: gf_copy(0, me, d).start())

    key_terms = [None] * (per_dev + 1)
    value_terms = [None] * (per_dev + 1)

    def put(terms, i, x):
        terms[i] = x if terms[i] is None else terms[i] + x

    def gb_copy(peer):
        return link(gbsend, gbbuf, gb_s, gb_r, "seq", peer)

    for g in range(per_dev):
        at = slice(g * blk, (g + 1) * blk)
        near = slice(g * blk, (g + 2) * blk)
        pn = wn[at, :] * inv_total[g]
        ga = grad_att[at, :]
        ds = (pn * (dot(ga, kvext[1, near, :], 1, 1) - delta[at, :])).astype(bf16)
        nk = dot(ds, q[at, :], 0, 0) * scale
        nv = dot(pn.astype(bf16), ga, 0, 0)
        for i in range(2):
            half = slice(i * blk, (i + 1) * blk)
            put(key_terms, g + i, nk[half, :])
            put(value_terms, g + i, nv[half, :])
        if g == 0:
            gbsend[0] = key_terms[0].astype(bf16)
            gbsend[1] = value_terms[0].astype(bf16)

            @pl.when(me > 0)
            def _():
                gb_copy(me - 1).start()

        gq[at, :] = (
            (dot(ds, kvext[0, near, :], 1, 0) + dot(dsf[at, :], kfar, 1, 0)) * scale
        ).astype(bf16)

    glk[...] = (mm(mix[...], lq[...], 0, 0) + mm(att[...], later, 1, 1)).astype(bf16)
    mixed[...] = (a32 + gain[...] * normed).astype(bf16)

    def take_gain(s, acc):
        gg_copy(s, s).wait_recv()
        return acc + ggbuf[s]

    gains = lax.fori_loop(0, me, take_gain, ggsend[...])
    gains = lax.fori_loop(me + 1, n, take_gain, gains)
    gg[...] = gains[0:1, :]

    @pl.when(me == n - 1)
    def _():
        gbbuf[...] = jnp.zeros_like(gbbuf)

    @pl.when(me < n - 1)
    def _():
        gb_copy(me + 1).wait_recv()

    zero = jnp.zeros((blk, width), f32)

    for side, terms, result in ((1, value_terms, gv), (0, key_terms, gk)):

        def take_far(s, acc):
            gf_copy(side, s, s).wait_recv()
            return acc + gfbuf[side, s].astype(f32)

        far = lax.fori_loop(me + 1, n, take_far, zero)
        for g in range(per_dev):
            x = terms[g + 1] + jnp.where(mine == g, far, 0.0)
            if g == per_dev - 1:
                x = x + gbbuf[side].astype(f32)
            result[g * blk : (g + 1) * blk, :] = x.astype(bf16)

    @pl.when(me < n - 1)
    def _():
        prev_copy(me + 1).wait_send()

    @pl.when(me > 0)
    def _():
        gb_copy(me - 1).wait_send()

    def sent_up(d):
        st_copy(me, d).wait_send()
        gg_copy(me, d).wait_send()

    def sent_down(d):
        gr_copy(me, d).wait_send()
        gf_copy(0, me, d).wait_send()
        gf_copy(1, me, d).wait_send()
        gg_copy(me, d).wait_send()

    loop(me + 1, n, sent_up)
    for side in range(2):
        loop(0, ahead, lambda i: kv_copy(side, me, me + 2 * (ahead - i)).wait_send())
        loop(0, pair, lambda i: kv_pass(side, me - 2 - 2 * i).wait_send())

        @pl.when(odd == 0)
        def _():
            kv_copy(side, me, me + 1).wait_send()

    loop(0, me, sent_down)
    loop(0, hd, lambda d: h_copy(hd, d).wait_send())
    loop(hd + 1, nh, lambda d: h_copy(hd, d).wait_send())


def hand_out(stacked, gains, *refs):
    sems = refs[7]
    copies = [
        pltpu.make_async_copy(stacked.at[pl.ds(i, 1)], refs[i], sems.at[i]) for i in range(6)
    ]
    copies.append(pltpu.make_async_copy(gains, refs[6], sems.at[6]))
    for copy in copies:
        copy.start()
    for copy in copies:
        copy.wait()


def per_device(query, key, value, lin_query, lin_key, gain, cotangent, key_block):
    heads, rows, width = query.shape
    n = lax.axis_size("seq")
    nh = lax.axis_size("head")
    blk = BLK
    flat = lambda x: x.reshape(heads * rows, width)
    vm = pl.BlockSpec(memory_space=pltpu.VMEM)
    hbm = pl.BlockSpec(memory_space=pl.ANY)
    total = jax.ShapeDtypeStruct((1, width), f32)
    dma = pltpu.SemaphoreType.DMA
    stacked, gains = pl.pallas_call(
        functools.partial(kernel, n, nh, width ** (-0.5)),
        out_shape=[jax.ShapeDtypeStruct((6, rows, width), bf16), total],
        in_specs=[vm] * 7 + [pl.BlockSpec(memory_space=pltpu.SMEM), vm],
        out_specs=[vm] * 2,
        scratch_shapes=[
            pltpu.VMEM((2, blk, width), bf16),
            pltpu.VMEM((2, n, blk, width), bf16),
            pltpu.VMEM((2, rows + blk, width), bf16),
            pltpu.VMEM((width, width), bf16),
            pltpu.VMEM((n, width, width), bf16),
            pltpu.VMEM((width, width), bf16),
            pltpu.VMEM((n, width, width), bf16),
            pltpu.VMEM((8, rows), f32),
            pltpu.VMEM((nh, 8, rows), f32),
            pltpu.VMEM((8, width), f32),
            pltpu.VMEM((n, 8, width), f32),
            pltpu.VMEM((2, n, blk, width), bf16),
            pltpu.VMEM((2, n, blk, width), bf16),
            pltpu.VMEM((2, blk, width), bf16),
            pltpu.VMEM((2, blk, width), bf16),
            pltpu.VMEM((rows, width), bf16),
            pltpu.VMEM((rows, 2 * blk), f32),
            pltpu.VMEM((rows, n * blk), f32),
            pltpu.VMEM((rows, n * blk), bf16),
            pltpu.VMEM((rows, n * blk), bf16),
            pltpu.VMEM((rows, rows), f32),
            dma((2, n)), dma((2, n)), dma, dma,
            dma((n,)), dma((n,)), dma((n,)), dma((n,)),
            dma((nh,)), dma((nh,)), dma((n,)), dma((n,)),
            dma((2, n)), dma((2, n)), dma, dma, dma((2, n)),
        ],
        compiler_params=pltpu.CompilerParams(
            collective_id=0, has_side_effects=True, vmem_limit_bytes=56 * 2**20
        ),
    )(
        flat(query), flat(key), flat(value), flat(lin_query), flat(lin_key), gain,
        flat(cotangent), key_block.T, key_block.T,
    )
    return tuple(
        pl.pallas_call(
            hand_out,
            out_shape=[jax.ShapeDtypeStruct((heads, rows, width), bf16)] * 6 + [total],
            in_specs=[hbm] * 2,
            out_specs=[vm] * 7,
            scratch_shapes=[dma((7,))],
        )(stacked, gains)
    )


def solution(mesh):
    split = P("head", "seq", None)
    return jax.shard_map(
        per_device,
        mesh=mesh,
        in_specs=(split,) * 5 + (P("head", None), split, P()),
        out_specs=(split,) * 6 + (P("head", None),),
        check_vma=False,
    )
```
